32 devices in a mesh: expert: 16 (over z, y, core), replica: 2 (over x).
Axes of the slice: x: 2, y: 2, z: 4, core: 2. Of those that a mesh axis runs over, the one named last changes fastest.
Arguments:
- grad_out: bfloat16 [1024, 2048], P(('expert', 'replica')), may hold values from -12 to 12
- routes: int32 [1024, 6], P(('expert', 'replica')), may hold values from 0 to 15, all different within a row; in each aligned block of 32 rows (0 to 31, 32 to 63, ...) at most 15 rows name the same one
- gates: float32 [1024, 6], P(('expert', 'replica')), may hold values from 0.03 to 0.6
- w_gate: bfloat16 [16, 1408, 2048], P('expert', 'replica'), may hold values from -0.125 to 0.125
- w_up: bfloat16 [16, 1408, 2048], P('expert', 'replica'), may hold values from -0.125 to 0.125
- w_down: bfloat16 [16, 1408, 2048], P('expert', 'replica'), may hold values from -0.15625 to 0.15625
- saved_gate: bfloat16 [16, 2, 16, 15, 1408], P('expert', 'replica'), may hold values from -8 to 8
- saved_up: bfloat16 [16, 2, 16, 15, 1408], P('expert', 'replica'), may hold values from -6 to 6
Outputs:
- grad_in: bfloat16 [1024, 2048], P(('expert', 'replica'))
The draws below stay inside these ranges and needn't reach their ends.
Inputs may be any that keep to these rules, and one draw needn't show every extreme that they name: `routes`: among the 32 tokens of one device, at most 15 entries name one expert; some expert is named 15 times; the 6 entries of a token differ.
All inputs are finite; a program needn't handle non-finite values.
Results may differ from the reference program's by a relative error of at most 0.01.
Values may be sent and summed in bfloat16 or wider, within the bound.
A program may use at most 128 MiB of HBM per device.

```python
import math
import jax
import jax.numpy as jnp
import numpy as np
from jax import lax

D = 2048
HID = 1408
TOP = 6
TOK_DEV = 32
EXPERTS = 16
TOKENS = 1024
CAP = 15
N_EXPERT = 16
N_REPLICA = 2


def block_levels(rng, dims, split, low, top_value):
    factor_of = 1.0
    for dim, blocks in split:
        draws = jax.random.uniform(jax.random.fold_in(jax.random.fold_in(rng, 6), dim), (blocks,), jnp.float32, low / len(split), top_value / len(split))
        factor_of = factor_of * jnp.repeat(jnp.exp(draws), dims[dim] // blocks).reshape((-1,) + (1,) * (len(dims) - 1 - dim))
    return factor_of


def shared_out(key, own, number, rows, amount, top, bound, lean):
    sequence = jax.random.permutation(key, amount)
    crowded, common = portions_of(amount, rows * top, bound, lean, True), portions_of(amount, rows * top, bound, lean, False)
    places = jnp.arange(amount)

    def named(sizes, offset_by):
        used = int((sizes > 0).sum())
        fixed = max(1, used // 4)
        passed = fixed + (places - fixed + offset_by * (used - fixed)) % max(1, amount - fixed)
        return jnp.zeros((amount,), jnp.int32).at[sequence[jnp.where(places < fixed, places, passed)]].set(jnp.asarray(sizes, jnp.int32))

    sizes = jnp.where(number % 4 == 0, named(crowded, number // 4), named(common, number - number // 4 - 1))
    mixed = jax.random.permutation(jax.random.fold_in(own, 3), amount)
    giver, receiver = mixed[0:amount // 2 * 2:2], mixed[1:amount // 2 * 2:2]
    slack = jnp.minimum(sizes[giver] - 1, bound - sizes[receiver]) // 2
    slack = jnp.where((giver == sequence[0]) | (receiver == sequence[0]) | (sizes[receiver] == 0), 0, jnp.maximum(slack, 0))
    passed = jax.random.randint(jax.random.fold_in(own, 4), (amount // 2,), 0, 1 << 20) % (slack + 1)
    sizes = sizes.at[giver].add(-passed).at[receiver].add(passed)
    items = jnp.searchsorted(jnp.cumsum(sizes), jnp.arange(rows * top), side="right").astype(jnp.int32)
    table = items.reshape(top, rows).T
    table = table[jax.random.permutation(jax.random.fold_in(own, 1), rows)]
    offset_by = jax.random.randint(jax.random.fold_in(own, 2), (rows, 1), 0, top)
    return jnp.take_along_axis(table, (jnp.arange(top)[None, :] + offset_by) % top, axis=1)


def portions_of(number_of, total, reach, skew, full):
    weights = [(1 << 20) // math.isqrt(standing ** skew) + 1 for standing in range(1, number_of + 1)]
    largest = reach if full else min(reach, max(-(-total // number_of), total * weights[0] // sum(weights)))
    least = 1 if total - largest >= number_of - 1 else 0
    given, rest = [largest] + [least] * (number_of - 1), total - largest - least * (number_of - 1)
    while rest > 0:
        movable = [i for i in range(1, number_of) if given[i] < largest] or [i for i in range(1, number_of) if given[i] < reach]
        whole, budget = sum([weights[i] for i in movable]), rest
        for i in movable:
            extra = min(reach - given[i], max(1, budget * weights[i] // whole), rest)
            given[i] = given[i] + extra
            rest = rest - extra
    return np.array(given)


def scatter_about(stream_key, shape, deviation, most, split=(), kind=jnp.bfloat16):
    values = deviation * jax.random.normal(stream_key, shape, jnp.float32)
    if split:
        values = values * block_levels(stream_key, shape, split, -0.22, 0.18)
    return jnp.clip(values, -most, most).astype(kind)


def setup_inputs(seed: int = 0) -> dict:
    key_list = jax.random.split(jax.random.key(seed), 9)
    grad_out = scatter_about(key_list[0], (TOKENS, D), 2.0, 12.0, ((0, 32),))
    routes_keys = jax.random.split(jax.random.fold_in(key_list[1], 1), TOKENS // TOK_DEV)
    routes_turns = jax.random.permutation(jax.random.fold_in(key_list[1], 3), TOKENS // TOK_DEV)
    routes = jax.vmap(lambda own, number: shared_out(jax.random.fold_in(key_list[1], 2), own, number, TOK_DEV, EXPERTS, TOP, CAP, 2))(routes_keys, routes_turns).reshape((TOKENS, TOP))
    gates = jnp.clip(jnp.exp(math.log(0.6) - 2.9957323 * jax.random.uniform(key_list[2], (TOKENS, TOP), jnp.float32) ** block_levels(key_list[2], (TOKENS, TOP), ((0, 32),), -0.2, 0.2)), 0.03, 0.6)
    w_gate = scatter_about(key_list[3], (EXPERTS, HID, D), D ** -0.5, 0.125, ((0, 16), (1, 2)))
    w_up = scatter_about(key_list[4], (EXPERTS, HID, D), D ** -0.5, 0.125, ((0, 16), (1, 2)))
    w_down = scatter_about(key_list[5], (EXPERTS, HID, D), HID ** -0.5, 0.15625, ((0, 16), (1, 2)))
    saved_gate = scatter_about(key_list[6], (EXPERTS, N_REPLICA, N_EXPERT, CAP, HID), 1.5, 8.0, ((0, 16), (1, 2)))
    saved_up = scatter_about(key_list[7], (EXPERTS, N_REPLICA, N_EXPERT, CAP, HID), 1.0, 6.0, ((0, 16), (1, 2)))
    return {"grad_out": grad_out, "routes": routes, "gates": gates, "w_gate": w_gate, "w_up": w_up, "w_down": w_down, "saved_gate": saved_gate, "saved_up": saved_up}


def backward_rows(rows, saved_g, saved_u, gate_w, up_w, down_w):
    hidden_grad = lax.dot_general(rows, down_w, (((1,), (1,)), ((), ())), preferred_element_type=jnp.float32)
    gate_val = saved_g.astype(jnp.float32)
    up_val = saved_u.astype(jnp.float32)
    sigma = jax.nn.sigmoid(gate_val)
    up_grad = (hidden_grad * gate_val * sigma).astype(jnp.bfloat16)
    gate_grad = (hidden_grad * up_val * sigma * (1.0 + gate_val * (1.0 - sigma))).astype(jnp.bfloat16)
    return jnp.dot(gate_grad, gate_w, preferred_element_type=jnp.float32) + jnp.dot(up_grad, up_w, preferred_element_type=jnp.float32)


def reference(grad_out, routes, gates, w_gate, w_up, w_down, saved_gate, saved_up):
    blocks = N_EXPERT * N_REPLICA
    entries = TOK_DEV * TOP
    width_slice = HID // N_REPLICA
    flat = routes.reshape(blocks, entries).astype(jnp.int32)
    labels = jnp.arange(EXPERTS, dtype=jnp.int32)
    hot = (flat[:, :, None] == labels[None, None, :]).astype(jnp.int32)
    position = jnp.sum((jnp.cumsum(hot, axis=1) - hot) * hot, axis=2).astype(jnp.int32)
    block_id = jnp.arange(blocks, dtype=jnp.int32)[:, None] * jnp.ones((1, entries), jnp.int32)
    group = (block_id % N_REPLICA).astype(jnp.int32)
    source = (block_id // N_REPLICA).astype(jnp.int32)
    scaled = (gates[:, :, None] * grad_out[:, None, :].astype(jnp.float32)).astype(jnp.bfloat16)
    scaled = scaled.reshape(blocks, entries, D)
    buffer = jnp.zeros((EXPERTS, N_REPLICA, N_EXPERT, CAP, D), jnp.bfloat16)
    buffer = buffer.at[flat, group, source, position].set(scaled)

    def one_expert(items):
        rows, gate_w, up_w, down_w, saved_g, saved_u = items
        rows = rows.reshape(-1, D)
        saved_g = saved_g.reshape(-1, HID)
        saved_u = saved_u.reshape(-1, HID)
        total = jnp.zeros((rows.shape[0], D), jnp.float32)
        for index in range(N_REPLICA):
            low = index * width_slice
            high = low + width_slice
            term = backward_rows(rows, saved_g[:, low:high], saved_u[:, low:high], gate_w[low:high], up_w[low:high], down_w[low:high])
            rounded = lax.optimization_barrier(term.astype(jnp.bfloat16))
            total = total + rounded.astype(jnp.float32)
        return total.astype(jnp.bfloat16)

    results = lax.map(one_expert, (buffer, w_gate, w_up, w_down, saved_gate, saved_up))
    results = results.reshape(EXPERTS, N_REPLICA, N_EXPERT, CAP, D)
    picked = results[flat, group, source, position]
    summed = jnp.sum(picked.astype(jnp.float32).reshape(TOKENS, TOP, D), axis=1)
    return summed.astype(jnp.bfloat16)
```

```python
import jax
import jax.numpy as jnp
from jax import lax
from jax.sharding import PartitionSpec as P


def backward_rows(rows, saved_g, saved_u, gate_w, up_w, down_w):
    hidden_grad = lax.dot_general(
        rows, down_w, (((1,), (1,)), ((), ())), preferred_element_type=jnp.float32
    )
    gate_val = saved_g.astype(jnp.float32)
    up_val = saved_u.astype(jnp.float32)
    sigma = jax.nn.sigmoid(gate_val)
    up_grad = (hidden_grad * gate_val * sigma).astype(jnp.bfloat16)
    gate_grad = (hidden_grad * up_val * sigma * (1.0 + gate_val * (1.0 - sigma))).astype(
        jnp.bfloat16
    )
    return jnp.dot(gate_grad, gate_w, preferred_element_type=jnp.float32) + jnp.dot(
        up_grad, up_w, preferred_element_type=jnp.float32
    )


def body(grad_out, routes, gates, w_gate, w_up, w_down, saved_gate, saved_up):
    experts = lax.axis_size("expert")
    tokens, width = grad_out.shape
    top = routes.shape[1]
    slots = saved_gate.shape[3]
    entries = tokens * top
    flat = routes.reshape(entries)
    labels = jnp.arange(experts, dtype=jnp.int32)
    hot = (flat[:, None] == labels[None, :]).astype(jnp.int32)
    position = jnp.sum((jnp.cumsum(hot, axis=0) - hot) * hot, axis=1)
    target = flat * slots + position
    placing = (jnp.arange(experts * slots, dtype=jnp.int32)[:, None] == target[None, :]).astype(
        jnp.bfloat16
    )
    scaled = (
        (gates[:, :, None] * grad_out[:, None, :].astype(jnp.float32))
        .astype(jnp.bfloat16)
        .reshape(entries, width)
    )
    outgoing = jnp.dot(placing, scaled, preferred_element_type=jnp.float32).astype(jnp.bfloat16)
    outgoing = outgoing.reshape(experts, slots, width)
    arrived = lax.all_to_all(outgoing, "expert", split_axis=0, concat_axis=0, tiled=True)
    sources = arrived.shape[0] * slots
    own_rows = arrived.reshape(sources, width)
    shared = (
        lax.all_to_all(saved_gate[0], "replica", split_axis=3, concat_axis=0, tiled=True),
        lax.all_to_all(saved_up[0], "replica", split_axis=3, concat_axis=0, tiled=True),
    )
    groups = shared[0].shape[0]
    shared_width = shared[0].shape[3]
    all_g = shared[0].reshape(groups * sources, shared_width)
    all_u = shared[1].reshape(groups * sources, shared_width)
    partials = backward_rows(
        lax.all_gather(own_rows, "replica", axis=0, tiled=True),
        all_g,
        all_u,
        w_gate[0],
        w_up[0],
        w_down[0],
    ).astype(jnp.bfloat16)
    partials = partials.reshape(groups, experts, slots, width)
    back = lax.all_to_all(
        lax.all_to_all(partials, "expert", split_axis=1, concat_axis=1, tiled=True),
        "replica",
        split_axis=0,
        concat_axis=0,
        tiled=True,
    )
    returned = jnp.sum(back, axis=0, dtype=jnp.float32).astype(jnp.bfloat16)
    combining = jnp.sum(placing.reshape(experts * slots, tokens, top), axis=2)
    summed = lax.dot_general(
        combining,
        returned.reshape(experts * slots, width),
        (((0,), (0,)), ((), ())),
        preferred_element_type=jnp.float32,
    )
    return summed.astype(jnp.bfloat16)


def token_meta(routes, gates, experts):
    labels = jnp.arange(experts, dtype=jnp.int32)
    hot = routes[:, :, None] == labels[None, None, :]
    named = jnp.any(hot, axis=1)
    count = named.astype(jnp.int32)
    code = jnp.where(named, jnp.cumsum(count, axis=0), 0).astype(jnp.bfloat16)
    gate = jnp.sum(jnp.where(hot, gates[:, :, None], 0.0), axis=1)
    high = lax.reduce_precision(gate, 8, 7)
    low = (gate - high).astype(jnp.bfloat16)
    return jnp.concatenate([code, high.astype(jnp.bfloat16), low], axis=1)


def gathered_body(grad_out, routes, gates, w_gate, w_up, w_down, saved_gate, saved_up):
    experts = lax.axis_size("expert")
    replicas = lax.axis_size("replica")
    tokens, width = grad_out.shape
    slots = saved_gate.shape[3]
    both = ("expert", "replica")
    meta = token_meta(routes, gates, experts)
    meta = jnp.pad(meta, ((0, 0), (0, -meta.shape[1] % 128)))
    packed = lax.all_gather(jnp.concatenate([grad_out, meta], axis=1), both, axis=0, tiled=True)
    shared = lax.all_to_all(
        jnp.stack([saved_gate[0, 0], saved_up[0, 0]]), "replica", split_axis=3, concat_axis=1, tiled=True
    )
    share = shared.shape[3]
    shared = shared.reshape(2, replicas, experts, slots, share).swapaxes(1, 2)
    shared = shared.reshape(2, experts * replicas * slots, share)
    me = lax.axis_index("expert")
    column = lambda k: lax.dynamic_slice_in_dim(packed, width + k * experts + me, 1, 1)[:, 0]
    code = column(0).astype(jnp.int32)
    gate = column(1).astype(jnp.float32) + column(2).astype(jnp.float32)
    blocks = experts * replicas
    scaled = (gate[:, None] * packed[:, :width].astype(jnp.float32)).astype(jnp.bfloat16)
    block = jnp.arange(blocks * tokens, dtype=jnp.int32) // tokens
    target = jnp.where(code > 0, block * slots + code - 1, -1)
    placing = (jnp.arange(blocks * slots, dtype=jnp.int32)[:, None] == target[None, :]).astype(jnp.bfloat16)
    rows = jnp.dot(placing, scaled, preferred_element_type=jnp.float32).astype(jnp.bfloat16)
    part = backward_rows(rows, shared[0], shared[1], w_gate[0], w_up[0], w_down[0]).astype(jnp.bfloat16)
    mine = lax.dot_general(placing, part, (((0,), (0,)), ((), ())), preferred_element_type=jnp.float32)
    return lax.psum_scatter(mine.astype(jnp.bfloat16), both, scatter_dimension=0, tiled=True)


def solution(mesh):
    in_specs = (
        P(("expert", "replica"), None),
        P(("expert", "replica"), None),
        P(("expert", "replica"), None),
        P("expert", "replica", None),
        P("expert", "replica", None),
        P("expert", "replica", None),
        P("expert", "replica", None, None, None),
        P("expert", "replica", None, None, None),
    )
    out_specs = P(("expert", "replica"), None)
    small = mesh.shape["replica"] == 2 and mesh.shape["expert"] <= 16
    return jax.shard_map(gathered_body if small else body, mesh=mesh, in_specs=in_specs, out_specs=out_specs, check_vma=False)
```

```python
import functools

import jax
import jax.numpy as jnp
from jax import lax
from jax.experimental import pallas as pl
from jax.experimental.pallas import tpu as pltpu
from jax.sharding import PartitionSpec as P


def backward_rows(rows, saved_g, saved_u, gate_w, up_w, down_w):
    hidden_grad = lax.dot_general(
        rows, down_w, (((1,), (1,)), ((), ())), preferred_element_type=jnp.float32
    )
    gate_val = saved_g.astype(jnp.float32)
    up_val = saved_u.astype(jnp.float32)
    sigma = jax.nn.sigmoid(gate_val)
    up_grad = (hidden_grad * gate_val * sigma).astype(jnp.bfloat16)
    gate_grad = (hidden_grad * up_val * sigma * (1.0 + gate_val * (1.0 - sigma))).astype(
        jnp.bfloat16
    )
    return jnp.dot(gate_grad, gate_w, preferred_element_type=jnp.float32) + jnp.dot(
        up_grad, up_w, preferred_element_type=jnp.float32
    )


def body(grad_out, routes, gates, w_gate, w_up, w_down, saved_gate, saved_up):
    experts = lax.axis_size("expert")
    tokens, width = grad_out.shape
    top = routes.shape[1]
    slots = saved_gate.shape[3]
    entries = tokens * top
    flat = routes.reshape(entries)
    labels = jnp.arange(experts, dtype=jnp.int32)
    hot = (flat[:, None] == labels[None, :]).astype(jnp.int32)
    position = jnp.sum((jnp.cumsum(hot, axis=0) - hot) * hot, axis=1)
    target = flat * slots + position
    placing = (jnp.arange(experts * slots, dtype=jnp.int32)[:, None] == target[None, :]).astype(
        jnp.bfloat16
    )
    scaled = (
        (gates[:, :, None] * grad_out[:, None, :].astype(jnp.float32))
        .astype(jnp.bfloat16)
        .reshape(entries, width)
    )
    outgoing = jnp.dot(placing, scaled, preferred_element_type=jnp.float32).astype(jnp.bfloat16)
    outgoing = outgoing.reshape(experts, slots, width)
    arrived = lax.all_to_all(outgoing, "expert", split_axis=0, concat_axis=0, tiled=True)
    sources = arrived.shape[0] * slots
    own_rows = arrived.reshape(sources, width)
    shared = (
        lax.all_to_all(saved_gate[0], "replica", split_axis=3, concat_axis=0, tiled=True),
        lax.all_to_all(saved_up[0], "replica", split_axis=3, concat_axis=0, tiled=True),
    )
    groups = shared[0].shape[0]
    shared_width = shared[0].shape[3]
    all_g = shared[0].reshape(groups * sources, shared_width)
    all_u = shared[1].reshape(groups * sources, shared_width)
    partials = backward_rows(
        lax.all_gather(own_rows, "replica", axis=0, tiled=True),
        all_g,
        all_u,
        w_gate[0],
        w_up[0],
        w_down[0],
    ).astype(jnp.bfloat16)
    partials = partials.reshape(groups, experts, slots, width)
    back = lax.all_to_all(
        lax.all_to_all(partials, "expert", split_axis=1, concat_axis=1, tiled=True),
        "replica",
        split_axis=0,
        concat_axis=0,
        tiled=True,
    )
    returned = jnp.sum(back, axis=0, dtype=jnp.float32).astype(jnp.bfloat16)
    combining = jnp.sum(placing.reshape(experts * slots, tokens, top), axis=2)
    summed = lax.dot_general(
        combining,
        returned.reshape(experts * slots, width),
        (((0,), (0,)), ((), ())),
        preferred_element_type=jnp.float32,
    )
    return summed.astype(jnp.bfloat16)


def token_meta(routes, gates, experts):
    labels = jnp.arange(experts, dtype=jnp.int32)
    hot = routes[:, :, None] == labels[None, None, :]
    named = jnp.any(hot, axis=1)
    count = named.astype(jnp.int32)
    code = jnp.where(named, jnp.cumsum(count, axis=0), 0).astype(jnp.bfloat16)
    gate = jnp.sum(jnp.where(hot, gates[:, :, None], 0.0), axis=1)
    high = lax.reduce_precision(gate, 8, 7)
    low = (gate - high).astype(jnp.bfloat16)
    return jnp.concatenate([code, high.astype(jnp.bfloat16), low], axis=1)


F32, BF16 = jnp.float32, jnp.bfloat16


def fused_kernel(
    planes, width, packed, saved, wg_hbm, wu_hbm, wd_hbm, out,
    tokens_all, acts, wg, wu, wd, mine, from_core, summed, from_b, line, from_z, final, from_a,
    local_sem, s_send, s_recv, a_send, a_recv, up_send, down_send, z_recv, b_send, b_recv, c_send, c_recv,
    rc_send, rc_recv, rb_send, rb_recv, rz_send, rz_recv, ra_send, ra_recv,
):
    expert, x = lax.axis_index("expert"), lax.axis_index("replica")
    c, y, z = expert % 2, (expert // 2) % 2, expert // 4
    packed_width = packed.shape[1]
    experts = planes * 4
    other_x, other_y = (expert, 1 - x), (expert + 2 - 4 * y, x)
    sibling, above, below = (expert + 1 - 2 * c, x), (expert + 4, x), (expert - 4, x)
    has_above, has_below = z < planes - 1, z > 0
    near, far = (other_x, other_y), (other_y, other_x)
    a_of, b_of = (x, y), (y, x)
    cut = (width * 14 // 16) // 128 * 128
    gather_cols = (pl.ds(0, cut), pl.ds(cut, packed_width - cut))
    half = width // 2
    cols = (pl.ds(0, half), pl.ds(half, half))

    def remote(src, dst, send, recv, device):
        return pltpu.make_async_remote_copy(
            src_ref=src, dst_ref=dst, send_sem=send, recv_sem=recv, device_id=device, device_id_type=pl.DeviceIdType.MESH
        )

    def one(s, plane, a):
        b = b_of[s]
        i, j = (b, a) if s == 0 else (a, b)
        return tokens_all.at[plane, i, c, j, :, gather_cols[s]]

    def pair(ref, s, plane, b, which):
        if len(ref.shape) == 6:
            return ref.at[plane, b, c, :, :, which] if s == 0 else ref.at[plane, :, c, b, :, which]
        return ref.at[plane, b, :, :, which] if s == 0 else ref.at[plane, :, b, :, which]

    def a_copy(s):
        r = one(s, z, a_of[s])
        return remote(r, r, a_send.at[s], a_recv.at[s], near[s])

    def z_block(s, q, plane):
        return one(s, plane, a_of[s] if q == 0 else 1 - a_of[s])

    def up_copy(s, q, plane):
        r = z_block(s, q, plane)
        return remote(r, r, up_send.at[s, q, plane], z_recv.at[s, q, plane], above)

    def down_copy(s, q, plane):
        r = z_block(s, q, plane)
        return remote(r, r, down_send.at[s, q, plane], z_recv.at[s, q, plane], below)

    def b_copy(s, plane):
        r = pair(tokens_all, s, plane, b_of[s], gather_cols[s])
        return remote(r, r, b_send.at[s, plane], b_recv.at[s, plane], far[s])

    def c_copy(plane):
        r = tokens_all.at[plane, :, c]
        return remote(r, r, c_send.at[plane], c_recv.at[plane], sibling)

    def saved_copy():
        return remote(saved.at[1 - x], acts.at[:, :, x], s_send, s_recv, other_x)

    def rc_copy(plane):
        return remote(mine.at[plane, :, 1 - c], from_core.at[plane], rc_send.at[plane], rc_recv.at[plane], sibling)

    def rb_copy(s, plane):
        src = pair(summed, s, plane, 1 - b_of[s], cols[s])
        return remote(src, from_b.at[plane, :, :, cols[s]], rb_send.at[s, plane], rb_recv.at[s, plane], far[s])

    def rz_copy(s, plane, up):
        slot = plane if up else jnp.where(plane == z - 1, planes, plane)
        return remote(
            line.at[plane, :, :, cols[s]], from_z.at[slot, :, :, cols[s]],
            rz_send.at[s, plane], rz_recv.at[s, slot], above if up else below,
        )

    def ra_copy(s):
        return remote(
            final.at[1 - a_of[s], :, cols[s]], from_a.at[:, cols[s]], ra_send.at[s], ra_recv.at[s], near[s]
        )

    def z_wait(s, slot):
        r = from_z.at[slot, :, :, cols[s]]
        pltpu.make_async_copy(r, r, rz_recv.at[s, slot]).wait()

    loads = [
        pltpu.make_async_copy(wd_hbm, wd, local_sem.at[0]),
        pltpu.make_async_copy(saved.at[x], acts.at[:, :, x], local_sem.at[1]),
        pltpu.make_async_copy(wg_hbm, wg, local_sem.at[2]),
        pltpu.make_async_copy(wu_hbm, wu, local_sem.at[3]),
    ]
    for load in loads:
        load.start()
    tokens_all[z, y, c, x] = packed[...]

    barrier = pltpu.get_barrier_semaphore()
    mesh_id = pl.DeviceIdType.MESH
    for device in (other_x, other_y, sibling):
        pl.semaphore_signal(barrier, inc=1, device_id=device, device_id_type=mesh_id)

    @pl.when(has_above)
    def _():
        pl.semaphore_signal(barrier, inc=1, device_id=above, device_id_type=mesh_id)

    @pl.when(has_below)
    def _():
        pl.semaphore_signal(barrier, inc=1, device_id=below, device_id_type=mesh_id)

    pl.semaphore_wait(barrier, 3 + has_above.astype(jnp.int32) + has_below.astype(jnp.int32))

    for s in range(2):
        a_copy(s).start()
    saved_copy().start()

    least = jnp.minimum(z, planes - 1 - z)

    def order(p):
        step = (p + 1) // 2
        swing = jnp.where(p % 2 == 1, z - step, z + step)
        rest = jnp.where(z < planes - 1 - z, z + (p - least), z - (p - least))
        return jnp.where(p <= 2 * least, swing, rest)

    def forward(plane):
        for q in range(2):
            for s in range(2):

                @pl.when(plane != z)
                def _():
                    r = z_block(s, q, plane)
                    pltpu.make_async_copy(r, r, z_recv.at[s, q, plane]).wait()

                if q == 1:

                    @pl.when(plane == z)
                    def _():
                        r = one(s, z, 1 - a_of[s])
                        pltpu.make_async_copy(r, r, a_recv.at[s]).wait()

                @pl.when((plane <= z) & has_above)
                def _():
                    up_copy(s, q, plane).start()

                @pl.when((plane >= z) & has_below)
                def _():
                    down_copy(s, q, plane).start()

        for s in range(2):
            b_copy(s, plane).start()

    def to_sibling(plane):
        for s in range(2):
            r = pair(tokens_all, s, plane, 1 - b_of[s], gather_cols[s])
            pltpu.make_async_copy(r, r, b_recv.at[s, plane]).wait()
        c_copy(plane).start()

    def compute(plane):
        r = tokens_all.at[plane, :, 1 - c]
        pltpu.make_async_copy(r, r, c_recv.at[plane]).wait()

        @pl.when(plane == z)
        def _():
            for load in loads:
                load.wait()
            r = acts.at[:, :, 1 - x]
            pltpu.make_async_copy(r, r, s_recv).wait()

        count = 8 * packed.shape[0]
        per = packed.shape[0]
        extra = packed_width - width
        rows = 2 * acts.shape[3]
        slots = rows // 8
        meta = tokens_all[plane, :, :, :, :, width:].reshape(count, extra)

        def placing(tokens_dim, lane_shape):
            def pick(k):
                if tokens_dim == 1:
                    chosen = lax.broadcasted_iota(jnp.int32, (rows, extra), 1) == k * experts + expert
                    return lax.dot_general(
                        chosen.astype(F32).astype(BF16), meta, (((1,), (1,)), ((), ())), preferred_element_type=F32
                    )
                chosen = lax.broadcasted_iota(jnp.int32, (extra, rows), 0) == k * experts + expert
                return jnp.dot(meta, chosen.astype(F32).astype(BF16), preferred_element_type=F32)

            code = pick(0).astype(jnp.int32)
            block = lax.broadcasted_iota(jnp.int32, lane_shape, tokens_dim) // per
            row = lax.broadcasted_iota(jnp.int32, lane_shape, 1 - tokens_dim)
            target = (block % 2) * (rows // 2) + (block // 2) * slots + code - 1
            return (code > 0) & (target == row), pick

        hot, pick = placing(1, (rows, count))
        high = jnp.where(hot, pick(1), 0.0).astype(BF16)
        low = jnp.where(hot, pick(2), 0.0).astype(BF16)
        hot_t, _ = placing(0, (count, rows))
        one_hot = jnp.where(hot_t, 1.0, 0.0).astype(BF16)
        tile = 512
        hidden_grad = jnp.zeros((rows, wd.shape[0]), F32)
        for n in range(0, width, tile):
            values = tokens_all[plane, :, :, :, :, n : n + tile].reshape(count, tile)
            placed = jnp.dot(high, values, preferred_element_type=F32) + jnp.dot(
                low, values, preferred_element_type=F32
            )
            hidden_grad += lax.dot_general(
                placed.astype(BF16), wd[:, n : n + tile], (((1,), (1,)), ((), ())), preferred_element_type=F32
            )
        gate_val = acts[0, plane].reshape(rows, wd.shape[0]).astype(F32)
        up_val = acts[1, plane].reshape(rows, wd.shape[0]).astype(F32)
        sigma = 1.0 / (1.0 + jnp.exp(-gate_val))
        up_grad = (hidden_grad * gate_val * sigma).astype(BF16)
        gate_grad = (hidden_grad * up_val * sigma * (1.0 + gate_val * (1.0 - sigma))).astype(BF16)
        for n in range(0, width, tile):
            part = jnp.dot(gate_grad, wg[:, n : n + tile], preferred_element_type=F32) + jnp.dot(
                up_grad, wu[:, n : n + tile], preferred_element_type=F32
            )
            back = jnp.dot(one_hot, part.astype(BF16), preferred_element_type=F32)
            mine[plane, :, :, :, :, n : n + tile] = back.astype(BF16).reshape(2, 2, 2, per, tile)
        rc_copy(plane).start()

    def sum_cores(plane):
        r = from_core.at[plane]
        pltpu.make_async_copy(r, r, rc_recv.at[plane]).wait()
        for i in range(2):
            total = mine[plane, i, c].astype(F32) + from_core[plane, i].astype(F32)
            summed[plane, i] = total.astype(BF16)
        for s in range(2):
            rb_copy(s, plane).start()

    @pl.loop(0, planes + 3)
    def _(p):
        @pl.when(p < planes)
        def _():
            forward(order(p))

        @pl.when((p >= 1) & (p < planes + 1))
        def _():
            to_sibling(order(p - 1))

        @pl.when((p >= 2) & (p < planes + 2))
        def _():
            compute(order(p - 2))

        @pl.when(p >= 3)
        def _():
            sum_cores(order(p - 3))

    def from_far(s, plane):
        r = from_b.at[plane, :, :, cols[s]]
        pltpu.make_async_copy(r, r, rb_recv.at[s, plane]).wait()
        lo = s * half
        for a in range(2):
            own = summed[plane, b_of[s], a, :, lo : lo + half] if s == 0 else summed[plane, a, b_of[s], :, lo : lo + half]
            total = own.astype(F32) + from_b[plane, a, :, lo : lo + half].astype(F32)
            line[plane, a, :, lo : lo + half] = total.astype(BF16)

    def add(s, plane, slot):
        z_wait(s, slot)
        lo = s * half
        total = line[plane, :, :, lo : lo + half].astype(F32) + from_z[slot, :, :, lo : lo + half].astype(F32)
        line[plane, :, :, lo : lo + half] = total.astype(BF16)

    @pl.loop(0, planes - 1)
    def _(p):
        plane = order(planes - 1 - p)
        for s in range(2):
            from_far(s, plane)

            @pl.when(((plane < z) & has_above) | ((plane > z) & has_below))
            def _():
                add(s, plane, plane)

            @pl.when(plane > z)
            def _():
                rz_copy(s, plane, True).start()

            @pl.when(plane < z)
            def _():
                rz_copy(s, plane, False).start()

    for s in range(2):
        from_far(s, z)

        @pl.when(has_below)
        def _():
            add(s, z, z)

        @pl.when(has_above)
        def _():
            add(s, z, planes)

        lo = s * half
        final[:, :, lo : lo + half] = line[z, :, :, lo : lo + half]
        ra_copy(s).start()
    for s in range(2):
        r = from_a.at[:, cols[s]]
        pltpu.make_async_copy(r, r, ra_recv.at[s]).wait()
        lo = s * half
        total = final[a_of[s], :, lo : lo + half].astype(F32) + from_a[:, lo : lo + half].astype(F32)
        out[:, lo : lo + half] = total.astype(BF16)

    saved_copy().wait_send()
    for s in range(2):
        a_copy(s).wait_send()
        ra_copy(s).wait_send()

    @pl.loop(0, planes)
    def _(plane):
        c_copy(plane).wait_send()
        rc_copy(plane).wait_send()
        for s in range(2):
            b_copy(s, plane).wait_send()
            rb_copy(s, plane).wait_send()
            for q in range(2):

                @pl.when((plane <= z) & has_above)
                def _():
                    up_copy(s, q, plane).wait_send()

                @pl.when((plane >= z) & has_below)
                def _():
                    down_copy(s, q, plane).wait_send()

            @pl.when(plane > z)
            def _():
                rz_copy(s, plane, True).wait_send()

            @pl.when(plane < z)
            def _():
                rz_copy(s, plane, False).wait_send()


def fused_body(grad_out, routes, gates, w_gate, w_up, w_down, saved_gate, saved_up):
    experts = lax.axis_size("expert")
    tokens, width = grad_out.shape
    planes = experts // 4
    slots = saved_gate.shape[3]
    share = w_down.shape[1]
    meta = token_meta(routes, gates, experts)
    packed = jnp.concatenate([grad_out, jnp.pad(meta, ((0, 0), (0, -meta.shape[1] % 128)))], axis=1)
    room = slots + -slots % 16
    saved = jnp.stack([saved_gate[0, 0], saved_up[0, 0]])
    saved = jnp.pad(saved, ((0, 0), (0, 0), (0, room - slots), (0, 0))).reshape(2, planes, 4 * room, 2 * share)
    saved = jnp.stack([saved[..., :share], saved[..., share:]])
    wide = packed.shape[1]
    dma = pltpu.SemaphoreType.DMA
    anywhere = pl.BlockSpec(memory_space=pl.ANY)
    vmem = pl.BlockSpec(memory_space=pltpu.VMEM)
    return pl.pallas_call(
        functools.partial(fused_kernel, planes, width),
        out_shape=jax.ShapeDtypeStruct((tokens, width), BF16),
        in_specs=[vmem] + [anywhere] * 4,
        out_specs=vmem,
        scratch_shapes=[
            pltpu.VMEM((planes, 2, 2, 2, tokens, wide), BF16),
            pltpu.VMEM((2, planes, 2, 4 * room, share), BF16),
            pltpu.VMEM((share, width), BF16),
            pltpu.VMEM((share, width), BF16),
            pltpu.VMEM((share, width), BF16),
            pltpu.VMEM((planes, 2, 2, 2, tokens, width), BF16),
            pltpu.VMEM((planes, 2, 2, tokens, width), BF16),
            pltpu.VMEM((planes, 2, 2, tokens, width), BF16),
            pltpu.VMEM((planes, 2, tokens, width), BF16),
            pltpu.VMEM((planes, 2, tokens, width), BF16),
            pltpu.VMEM((planes + 1, 2, tokens, width), BF16),
            pltpu.VMEM((2, tokens, width), BF16),
            pltpu.VMEM((tokens, width), BF16),
            dma((4,)), dma, dma, dma((2,)), dma((2,)),
            dma((2, 2, planes)), dma((2, 2, planes)), dma((2, 2, planes)),
            dma((2, planes)), dma((2, planes)), dma((planes,)), dma((planes,)),
            dma((planes,)), dma((planes,)), dma((2, planes)), dma((2, planes)),
            dma((2, planes)), dma((2, planes + 1)), dma((2,)), dma((2,)),
        ],
        compiler_params=pltpu.CompilerParams(
            collective_id=0, has_side_effects=True, vmem_limit_bytes=48 * 2**20
        ),
    )(packed, saved, w_gate[0], w_up[0], w_down[0])


def solution(mesh):
    in_specs = (
        P(("expert", "replica"), None),
        P(("expert", "replica"), None),
        P(("expert", "replica"), None),
        P("expert", "replica", None),
        P("expert", "replica", None),
        P("expert", "replica", None),
        P("expert", "replica", None, None, None),
        P("expert", "replica", None, None, None),
    )
    out_specs = P(("expert", "replica"), None)
    small = mesh.shape["replica"] == 2 and mesh.shape["expert"] in (8, 16)
    return jax.shard_map(fused_body if small else body, mesh=mesh, in_specs=in_specs, out_specs=out_specs, check_vma=False)
```

```python
import functools

import jax
import jax.numpy as jnp
from jax import lax
from jax.experimental import pallas as pl
from jax.experimental.pallas import tpu as pltpu
from jax.sharding import PartitionSpec as P


def backward_rows(rows, saved_g, saved_u, gate_w, up_w, down_w):
    hidden_grad = lax.dot_general(
        rows, down_w, (((1,), (1,)), ((), ())), preferred_element_type=jnp.float32
    )
    gate_val = saved_g.astype(jnp.float32)
    up_val = saved_u.astype(jnp.float32)
    sigma = jax.nn.sigmoid(gate_val)
    up_grad = (hidden_grad * gate_val * sigma).astype(jnp.bfloat16)
    gate_grad = (hidden_grad * up_val * sigma * (1.0 + gate_val * (1.0 - sigma))).astype(
        jnp.bfloat16
    )
    return jnp.dot(gate_grad, gate_w, preferred_element_type=jnp.float32) + jnp.dot(
        up_grad, up_w, preferred_element_type=jnp.float32
    )


def body(grad_out, routes, gates, w_gate, w_up, w_down, saved_gate, saved_up):
    experts = lax.axis_size("expert")
    tokens, width = grad_out.shape
    top = routes.shape[1]
    slots = saved_gate.shape[3]
    entries = tokens * top
    flat = routes.reshape(entries)
    labels = jnp.arange(experts, dtype=jnp.int32)
    hot = (flat[:, None] == labels[None, :]).astype(jnp.int32)
    position = jnp.sum((jnp.cumsum(hot, axis=0) - hot) * hot, axis=1)
    target = flat * slots + position
    placing = (jnp.arange(experts * slots, dtype=jnp.int32)[:, None] == target[None, :]).astype(
        jnp.bfloat16
    )
    scaled = (
        (gates[:, :, None] * grad_out[:, None, :].astype(jnp.float32))
        .astype(jnp.bfloat16)
        .reshape(entries, width)
    )
    outgoing = jnp.dot(placing, scaled, preferred_element_type=jnp.float32).astype(jnp.bfloat16)
    outgoing = outgoing.reshape(experts, slots, width)
    arrived = lax.all_to_all(outgoing, "expert", split_axis=0, concat_axis=0, tiled=True)
    sources = arrived.shape[0] * slots
    own_rows = arrived.reshape(sources, width)
    shared = (
        lax.all_to_all(saved_gate[0], "replica", split_axis=3, concat_axis=0, tiled=True),
        lax.all_to_all(saved_up[0], "replica", split_axis=3, concat_axis=0, tiled=True),
    )
    groups = shared[0].shape[0]
    shared_width = shared[0].shape[3]
    all_g = shared[0].reshape(groups * sources, shared_width)
    all_u = shared[1].reshape(groups * sources, shared_width)
    partials = backward_rows(
        lax.all_gather(own_rows, "replica", axis=0, tiled=True),
        all_g,
        all_u,
        w_gate[0],
        w_up[0],
        w_down[0],
    ).astype(jnp.bfloat16)
    partials = partials.reshape(groups, experts, slots, width)
    back = lax.all_to_all(
        lax.all_to_all(partials, "expert", split_axis=1, concat_axis=1, tiled=True),
        "replica",
        split_axis=0,
        concat_axis=0,
        tiled=True,
    )
    returned = jnp.sum(back, axis=0, dtype=jnp.float32).astype(jnp.bfloat16)
    combining = jnp.sum(placing.reshape(experts * slots, tokens, top), axis=2)
    summed = lax.dot_general(
        combining,
        returned.reshape(experts * slots, width),
        (((0,), (0,)), ((), ())),
        preferred_element_type=jnp.float32,
    )
    return summed.astype(jnp.bfloat16)


def token_meta(routes, gates, experts):
    labels = jnp.arange(experts, dtype=jnp.int32)
    hot = routes[:, :, None] == labels[None, None, :]
    named = jnp.any(hot, axis=1)
    count = named.astype(jnp.int32)
    code = jnp.where(named, jnp.cumsum(count, axis=0), 0).astype(jnp.bfloat16)
    gate = jnp.sum(jnp.where(hot, gates[:, :, None], 0.0), axis=1)
    high = lax.reduce_precision(gate, 8, 7)
    low = (gate - high).astype(jnp.bfloat16)
    return jnp.concatenate([code, high.astype(jnp.bfloat16), low], axis=1)


F32, BF16 = jnp.float32, jnp.bfloat16


def fused_kernel(
    planes, width, packed, saved, wg_hbm, wu_hbm, wd_hbm, out,
    tokens_all, acts, wg, wu, wd, mine, from_core, summed, from_b, line, from_z, final, from_a,
    local_sem, s_send, s_recv, a_send, a_recv, up_send, down_send, z_recv, b_send, b_recv, c_send, c_recv,
    rc_send, rc_recv, rb_send, rb_recv, rz_send, rz_recv, ra_send, ra_recv,
):
    expert, x = lax.axis_index("expert"), lax.axis_index("replica")
    c, y, z = expert % 2, (expert // 2) % 2, expert // 4
    packed_width = packed.shape[1]
    experts = planes * 4
    other_x, other_y = (expert, 1 - x), (expert + 2 - 4 * y, x)
    sibling, above, below = (expert + 1 - 2 * c, x), (expert + 4, x), (expert - 4, x)
    has_above, has_below = z < planes - 1, z > 0
    near, far = (other_x, other_y), (other_y, other_x)
    a_of, b_of = (x, y), (y, x)
    cut = (width * 14 // 16) // 128 * 128
    gather_cols = (pl.ds(0, cut), pl.ds(cut, packed_width - cut))
    half = width // 2
    cols = (pl.ds(0, half), pl.ds(half, half))

    def remote(src, dst, send, recv, device):
        return pltpu.make_async_remote_copy(
            src_ref=src, dst_ref=dst, send_sem=send, recv_sem=recv, device_id=device, device_id_type=pl.DeviceIdType.MESH
        )

    def one(s, plane, a):
        b = b_of[s]
        i, j = (b, a) if s == 0 else (a, b)
        return tokens_all.at[plane, i, c, j, :, gather_cols[s]]

    def pair(ref, s, plane, b, which):
        if len(ref.shape) == 6:
            return ref.at[plane, b, c, :, :, which] if s == 0 else ref.at[plane, :, c, b, :, which]
        return ref.at[plane, b, :, :, which] if s == 0 else ref.at[plane, :, b, :, which]

    def a_copy(s):
        r = one(s, z, a_of[s])
        return remote(r, r, a_send.at[s], a_recv.at[s], near[s])

    def z_block(s, q, plane):
        return one(s, plane, a_of[s] if q == 0 else 1 - a_of[s])

    def up_copy(s, q, plane):
        r = z_block(s, q, plane)
        return remote(r, r, up_send.at[s, q, plane], z_recv.at[s, q, plane], above)

    def down_copy(s, q, plane):
        r = z_block(s, q, plane)
        return remote(r, r, down_send.at[s, q, plane], z_recv.at[s, q, plane], below)

    def b_copy(s, plane):
        r = pair(tokens_all, s, plane, b_of[s], gather_cols[s])
        return remote(r, r, b_send.at[s, plane], b_recv.at[s, plane], far[s])

    def c_copy(plane):
        r = tokens_all.at[plane, :, c]
        return remote(r, r, c_send.at[plane], c_recv.at[plane], sibling)

    def saved_copy(plane):
        return remote(saved.at[1 - x, :, plane], acts.at[:, plane, x], s_send.at[plane], s_recv.at[plane], other_x)

    def rc_copy(plane):
        return remote(mine.at[plane, :, 1 - c], from_core.at[plane], rc_send.at[plane], rc_recv.at[plane], sibling)

    def rb_copy(s, plane):
        src = pair(summed, s, plane, 1 - b_of[s], cols[s])
        return remote(src, from_b.at[plane, :, :, cols[s]], rb_send.at[s, plane], rb_recv.at[s, plane], far[s])

    def rz_copy(s, plane, up):
        slot = plane if up else jnp.where(plane == z - 1, planes, plane)
        return remote(
            line.at[plane, :, :, cols[s]], from_z.at[slot, :, :, cols[s]],
            rz_send.at[s, plane], rz_recv.at[s, slot], above if up else below,
        )

    def ra_copy(s):
        return remote(
            final.at[1 - a_of[s], :, cols[s]], from_a.at[:, cols[s]], ra_send.at[s], ra_recv.at[s], near[s]
        )

    def z_wait(s, slot):
        r = from_z.at[slot, :, :, cols[s]]
        pltpu.make_async_copy(r, r, rz_recv.at[s, slot]).wait()

    loads = [
        pltpu.make_async_copy(wd_hbm, wd, local_sem.at[0]),
        pltpu.make_async_copy(saved.at[x], acts.at[:, :, x], local_sem.at[1]),
        pltpu.make_async_copy(wg_hbm, wg, local_sem.at[2]),
        pltpu.make_async_copy(wu_hbm, wu, local_sem.at[3]),
    ]
    for load in loads:
        load.start()
    tokens_all[z, y, c, x] = packed[...]

    barrier = pltpu.get_barrier_semaphore()
    mesh_id = pl.DeviceIdType.MESH
    for device in (other_x, other_y, sibling):
        pl.semaphore_signal(barrier, inc=1, device_id=device, device_id_type=mesh_id)

    @pl.when(has_above)
    def _():
        pl.semaphore_signal(barrier, inc=1, device_id=above, device_id_type=mesh_id)

    @pl.when(has_below)
    def _():
        pl.semaphore_signal(barrier, inc=1, device_id=below, device_id_type=mesh_id)

    pl.semaphore_wait(barrier, 3 + has_above.astype(jnp.int32) + has_below.astype(jnp.int32))

    for s in range(2):
        a_copy(s).start()
    least = jnp.minimum(z, planes - 1 - z)

    def order(p):
        step = (p + 1) // 2
        swing = jnp.where(p % 2 == 1, z - step, z + step)
        rest = jnp.where(z < planes - 1 - z, z + (p - least), z - (p - least))
        return jnp.where(p <= 2 * least, swing, rest)

    def forward(plane):
        for q in range(2):
            for s in range(2):

                @pl.when(plane != z)
                def _():
                    r = z_block(s, q, plane)
                    pltpu.make_async_copy(r, r, z_recv.at[s, q, plane]).wait()

                if q == 1:

                    @pl.when(plane == z)
                    def _():
                        r = one(s, z, 1 - a_of[s])
                        pltpu.make_async_copy(r, r, a_recv.at[s]).wait()

                @pl.when((plane <= z) & has_above)
                def _():
                    up_copy(s, q, plane).start()

                @pl.when((plane >= z) & has_below)
                def _():
                    down_copy(s, q, plane).start()

        for s in range(2):
            b_copy(s, plane).start()
        saved_copy(plane).start()

    def to_sibling(plane):
        for s in range(2):
            r = pair(tokens_all, s, plane, 1 - b_of[s], gather_cols[s])
            pltpu.make_async_copy(r, r, b_recv.at[s, plane]).wait()
        c_copy(plane).start()

    def compute(plane):
        r = tokens_all.at[plane, :, 1 - c]
        pltpu.make_async_copy(r, r, c_recv.at[plane]).wait()

        @pl.when(plane == z)
        def _():
            for load in loads:
                load.wait()

        r = acts.at[:, plane, 1 - x]
        pltpu.make_async_copy(r, r, s_recv.at[plane]).wait()

        count = 8 * packed.shape[0]
        per = packed.shape[0]
        extra = packed_width - width
        rows = 2 * acts.shape[3]
        slots = rows // 8
        meta = tokens_all[plane, :, :, :, :, width:].reshape(count, extra)

        def placing(tokens_dim, lane_shape):
            def pick(k):
                if tokens_dim == 1:
                    chosen = lax.broadcasted_iota(jnp.int32, (rows, extra), 1) == k * experts + expert
                    return lax.dot_general(
                        chosen.astype(F32).astype(BF16), meta, (((1,), (1,)), ((), ())), preferred_element_type=F32
                    )
                chosen = lax.broadcasted_iota(jnp.int32, (extra, rows), 0) == k * experts + expert
                return jnp.dot(meta, chosen.astype(F32).astype(BF16), preferred_element_type=F32)

            code = pick(0).astype(jnp.int32)
            block = lax.broadcasted_iota(jnp.int32, lane_shape, tokens_dim) // per
            row = lax.broadcasted_iota(jnp.int32, lane_shape, 1 - tokens_dim)
            target = (block % 2) * (rows // 2) + (block // 2) * slots + code - 1
            return (code > 0) & (target == row), pick

        hot, pick = placing(1, (rows, count))
        high = jnp.where(hot, pick(1), 0.0).astype(BF16)
        low = jnp.where(hot, pick(2), 0.0).astype(BF16)
        hot_t, _ = placing(0, (count, rows))
        one_hot = jnp.where(hot_t, 1.0, 0.0).astype(BF16)
        tile = 512
        hidden_grad = jnp.zeros((rows, wd.shape[0]), F32)
        for n in range(0, width, tile):
            values = tokens_all[plane, :, :, :, :, n : n + tile].reshape(count, tile)
            placed = jnp.dot(high, values, preferred_element_type=F32) + jnp.dot(
                low, values, preferred_element_type=F32
            )
            hidden_grad += lax.dot_general(
                placed.astype(BF16), wd[:, n : n + tile], (((1,), (1,)), ((), ())), preferred_element_type=F32
            )
        gate_val = acts[0, plane].reshape(rows, wd.shape[0]).astype(F32)
        up_val = acts[1, plane].reshape(rows, wd.shape[0]).astype(F32)
        sigma = 1.0 / (1.0 + jnp.exp(-gate_val))
        up_grad = (hidden_grad * gate_val * sigma).astype(BF16)
        gate_grad = (hidden_grad * up_val * sigma * (1.0 + gate_val * (1.0 - sigma))).astype(BF16)
        for n in range(0, width, tile):
            part = jnp.dot(gate_grad, wg[:, n : n + tile], preferred_element_type=F32) + jnp.dot(
                up_grad, wu[:, n : n + tile], preferred_element_type=F32
            )
            back = jnp.dot(one_hot, part.astype(BF16), preferred_element_type=F32)
            mine[plane, :, :, :, :, n : n + tile] = back.astype(BF16).reshape(2, 2, 2, per, tile)
        rc_copy(plane).start()

    def sum_cores(plane):
        r = from_core.at[plane]
        pltpu.make_async_copy(r, r, rc_recv.at[plane]).wait()
        for i in range(2):
            total = mine[plane, i, c].astype(F32) + from_core[plane, i].astype(F32)
            summed[plane, i] = total.astype(BF16)
        for s in range(2):
            rb_copy(s, plane).start()

    @pl.loop(0, planes + 3)
    def _(p):
        @pl.when(p < planes)
        def _():
            forward(order(p))

        @pl.when((p >= 1) & (p < planes + 1))
        def _():
            to_sibling(order(p - 1))

        @pl.when((p >= 2) & (p < planes + 2))
        def _():
            compute(order(p - 2))

        @pl.when(p >= 3)
        def _():
            sum_cores(order(p - 3))

    def from_far(s, plane):
        r = from_b.at[plane, :, :, cols[s]]
        pltpu.make_async_copy(r, r, rb_recv.at[s, plane]).wait()
        lo = s * half
        for a in range(2):
            own = summed[plane, b_of[s], a, :, lo : lo + half] if s == 0 else summed[plane, a, b_of[s], :, lo : lo + half]
            total = own.astype(F32) + from_b[plane, a, :, lo : lo + half].astype(F32)
            line[plane, a, :, lo : lo + half] = total.astype(BF16)

    def add(s, plane, slot):
        z_wait(s, slot)
        lo = s * half
        total = line[plane, :, :, lo : lo + half].astype(F32) + from_z[slot, :, :, lo : lo + half].astype(F32)
        line[plane, :, :, lo : lo + half] = total.astype(BF16)

    @pl.loop(0, planes - 1)
    def _(p):
        plane = order(planes - 1 - p)
        for s in range(2):
            from_far(s, plane)

            @pl.when(((plane < z) & has_above) | ((plane > z) & has_below))
            def _():
                add(s, plane, plane)

            @pl.when(plane > z)
            def _():
                rz_copy(s, plane, True).start()

            @pl.when(plane < z)
            def _():
                rz_copy(s, plane, False).start()

    for s in range(2):
        from_far(s, z)

        @pl.when(has_below)
        def _():
            add(s, z, z)

        @pl.when(has_above)
        def _():
            add(s, z, planes)

        lo = s * half
        final[:, :, lo : lo + half] = line[z, :, :, lo : lo + half]
        ra_copy(s).start()
    for s in range(2):
        r = from_a.at[:, cols[s]]
        pltpu.make_async_copy(r, r, ra_recv.at[s]).wait()
        lo = s * half
        total = final[a_of[s], :, lo : lo + half].astype(F32) + from_a[:, lo : lo + half].astype(F32)
        out[:, lo : lo + half] = total.astype(BF16)

    for s in range(2):
        a_copy(s).wait_send()
        ra_copy(s).wait_send()

    @pl.loop(0, planes)
    def _(plane):
        saved_copy(plane).wait_send()
        c_copy(plane).wait_send()
        rc_copy(plane).wait_send()
        for s in range(2):
            b_copy(s, plane).wait_send()
            rb_copy(s, plane).wait_send()
            for q in range(2):

                @pl.when((plane <= z) & has_above)
                def _():
                    up_copy(s, q, plane).wait_send()

                @pl.when((plane >= z) & has_below)
                def _():
                    down_copy(s, q, plane).wait_send()

            @pl.when(plane > z)
            def _():
                rz_copy(s, plane, True).wait_send()

            @pl.when(plane < z)
            def _():
                rz_copy(s, plane, False).wait_send()


def fused_body(grad_out, routes, gates, w_gate, w_up, w_down, saved_gate, saved_up):
    experts = lax.axis_size("expert")
    tokens, width = grad_out.shape
    planes = experts // 4
    slots = saved_gate.shape[3]
    share = w_down.shape[1]
    meta = token_meta(routes, gates, experts)
    packed = jnp.concatenate([grad_out, jnp.pad(meta, ((0, 0), (0, -meta.shape[1] % 128)))], axis=1)
    room = slots + -slots % 16
    saved = jnp.stack([saved_gate[0, 0], saved_up[0, 0]])
    saved = jnp.pad(saved, ((0, 0), (0, 0), (0, room - slots), (0, 0))).reshape(2, planes, 4 * room, 2 * share)
    saved = jnp.stack([saved[..., :share], saved[..., share:]])
    wide = packed.shape[1]
    dma = pltpu.SemaphoreType.DMA
    anywhere = pl.BlockSpec(memory_space=pl.ANY)
    vmem = pl.BlockSpec(memory_space=pltpu.VMEM)
    return pl.pallas_call(
        functools.partial(fused_kernel, planes, width),
        out_shape=jax.ShapeDtypeStruct((tokens, width), BF16),
        in_specs=[vmem] + [anywhere] * 4,
        out_specs=vmem,
        scratch_shapes=[
            pltpu.VMEM((planes, 2, 2, 2, tokens, wide), BF16),
            pltpu.VMEM((2, planes, 2, 4 * room, share), BF16),
            pltpu.VMEM((share, width), BF16),
            pltpu.VMEM((share, width), BF16),
            pltpu.VMEM((share, width), BF16),
            pltpu.VMEM((planes, 2, 2, 2, tokens, width), BF16),
            pltpu.VMEM((planes, 2, 2, tokens, width), BF16),
            pltpu.VMEM((planes, 2, 2, tokens, width), BF16),
            pltpu.VMEM((planes, 2, tokens, width), BF16),
            pltpu.VMEM((planes, 2, tokens, width), BF16),
            pltpu.VMEM((planes + 1, 2, tokens, width), BF16),
            pltpu.VMEM((2, tokens, width), BF16),
            pltpu.VMEM((tokens, width), BF16),
            dma((4,)), dma((planes,)), dma((planes,)), dma((2,)), dma((2,)),
            dma((2, 2, planes)), dma((2, 2, planes)), dma((2, 2, planes)),
            dma((2, planes)), dma((2, planes)), dma((planes,)), dma((planes,)),
            dma((planes,)), dma((planes,)), dma((2, planes)), dma((2, planes)),
            dma((2, planes)), dma((2, planes + 1)), dma((2,)), dma((2,)),
        ],
        compiler_params=pltpu.CompilerParams(
            collective_id=0, has_side_effects=True, vmem_limit_bytes=48 * 2**20
        ),
    )(packed, saved, w_gate[0], w_up[0], w_down[0])


def solution(mesh):
    in_specs = (
        P(("expert", "replica"), None),
        P(("expert", "replica"), None),
        P(("expert", "replica"), None),
        P("expert", "replica", None),
        P("expert", "replica", None),
        P("expert", "replica", None),
        P("expert", "replica", None, None, None),
        P("expert", "replica", None, None, None),
    )
    out_specs = P(("expert", "replica"), None)
    small = mesh.shape["replica"] == 2 and mesh.shape["expert"] in (8, 16)
    return jax.shard_map(fused_body if small else body, mesh=mesh, in_specs=in_specs, out_specs=out_specs, check_vma=False)
```
